32 devices in a mesh: groups: 2 (over y), clips: 4 (over z), tm: 2 (over x), chan: 2 (over core).
Axes of the slice: x: 2, y: 2, z: 4, core: 2. Of those that a mesh axis runs over, the one named last changes fastest.
Arguments:
- video: bfloat16 [4, 64, 4, 8, 128], P(('groups', 'tm'), 'clips', None, None, 'chan'), parts along dimension 0, may hold values from -6 to 6, as said below
- frame_owner: int32 [4, 64, 1], P(('groups', 'tm'), 'clips'), parts along dimension 0, may hold values from 0 to 3, as said below
- conv_first: bfloat16 [3, 3, 3, 128, 128], replicated, may hold values from -0.109375 to 0.109375
- conv_second: bfloat16 [3, 3, 3, 128, 128], replicated, may hold values from -0.109375 to 0.109375
Outputs:
- encoded: bfloat16 [4, 128, 4, 8, 128], P(('groups', 'tm'), 'clips', None, None, 'chan'), parts along dimension 0
The draws below stay inside these ranges and needn't reach their ends.
There are 2 independent parts, one for each index of `groups`. The reference program is written for one: setup_inputs(seed, part) draws one part's arguments, and reference() takes and returns one part's arrays. A program takes and returns all parts, laid end to end along the dimension named above; an argument that names none is the same for every part. Nothing has to cross between parts.
Inputs may be any that keep to these rules, and one draw needn't show every extreme that they name: `frame_owner`: in each aligned block of 16 rows (the frames of one reader device in one period) no owner is named more than 8 times, and in every block some owner exactly 8 times. A clip may have no frame, or a single frame, in a whole period, and may have no frame over several periods in a row. `video`: A stored frame may be black: all its entries zero.
All inputs are finite; a program needn't handle non-finite values.
Results may differ from the reference program's by a relative error of at most 0.0044.
Values may be sent and summed in bfloat16 or wider, within the bound.
A program may use at most 64 MiB of HBM per device.

```python
import jax
import jax.numpy as jnp
from jax import lax

C = 128
KT = 3
KS = 3
TILE_H = 4
TILE_W = 8
SLOTS = 16
CAP = 8
N_CLIPS = 4
N_TM = 2


def draw_video(key, part):
    keys = jax.random.split(key, 3)
    row_total = N_CLIPS * SLOTS
    full_shape = (N_TM, row_total, TILE_H, TILE_W, C)
    values = jnp.clip(jax.random.normal(keys[0], full_shape), -6.0, 6.0)
    black_rows = jax.random.randint(keys[2], (N_TM, 2), 0, row_total).astype(jnp.int32)
    row_ids = jnp.arange(row_total, dtype=jnp.int32)
    is_black = (row_ids[None, :] == black_rows[:, 0:1]) | (row_ids[None, :] == black_rows[:, 1:2])
    values = jnp.where(is_black[:, :, None, None, None], 0.0, values)
    return values.astype(jnp.float32).astype(jnp.bfloat16)


def draw_frame_owner(key, part):
    block_count = N_TM * N_CLIPS
    ticket_count = N_CLIPS * CAP
    keys = jax.random.split(key, 9)
    silent_clip = jax.random.randint(keys[7], (), 0, N_CLIPS).astype(jnp.int32)
    periods = jnp.arange(N_TM, dtype=jnp.int32)
    middle = (periods >= 1) & (periods <= N_TM - 2)
    other_absent = ((silent_clip + 1 + jax.random.randint(keys[0], (N_TM,), 0, N_CLIPS - 1)) % N_CLIPS).astype(jnp.int32)
    absent = jnp.where(middle, silent_clip, other_absent).astype(jnp.int32)
    single = ((absent + 1 + jax.random.randint(keys[1], (N_TM,), 0, N_CLIPS - 1)) % N_CLIPS).astype(jnp.int32)
    single_reader = jax.random.randint(keys[2], (N_TM,), 0, N_CLIPS).astype(jnp.int32)
    rank_draw = jax.random.randint(keys[3], (N_TM, N_CLIPS), 0, 1 << 20)
    owner_rank = jnp.argsort(jnp.argsort(rank_draw, axis=1, stable=True), axis=1, stable=True)
    weight = (256 // (1 + owner_rank)).astype(jnp.int32)
    block_ids = jnp.arange(block_count, dtype=jnp.int32)
    period_of = block_ids // N_CLIPS
    reader_of = block_ids % N_CLIPS
    owner_ids = jnp.arange(N_CLIPS, dtype=jnp.int32)
    qualified_mask = (owner_ids[None, :] != absent[period_of][:, None]) & (owner_ids[None, :] != single[period_of][:, None])
    block_weight = weight[period_of]
    level = jax.random.randint(keys[4], (block_count, N_CLIPS), 0, 256).astype(jnp.int32) * block_weight
    level = jnp.where(qualified_mask, level, -1)
    loaded_owner = jnp.argsort(-level, axis=1, stable=True)[:, 0].astype(jnp.int32)
    forced_reader = jax.random.randint(keys[8], (N_TM,), 0, N_CLIPS).astype(jnp.int32)
    force_block = jnp.logical_not(middle[period_of]) & (reader_of == forced_reader[period_of]) & (single[period_of] != silent_clip)
    loaded_owner = jnp.where(force_block, silent_clip, loaded_owner).astype(jnp.int32)
    voucher_holder = jnp.arange(ticket_count, dtype=jnp.int32) // CAP
    starting_offset = jax.random.randint(keys[5], (block_count, ticket_count), 0, 256).astype(jnp.int32) * block_weight[:, voucher_holder]
    extra_credit = jnp.where(voucher_holder[None, :] == loaded_owner[:, None], 1 << 20, 0)
    owner_rating = jnp.where(qualified_mask[:, voucher_holder], starting_offset + extra_credit, -1)
    order = jnp.argsort(-owner_rating, axis=1, stable=True)
    chosen = voucher_holder[order[:, :SLOTS]].astype(jnp.int32)
    is_single = reader_of == single_reader[period_of]
    last_owner = jnp.where(is_single, single[period_of], chosen[:, SLOTS - 1]).astype(jnp.int32)
    chosen = chosen.at[:, SLOTS - 1].set(last_owner)
    shuffle = jnp.argsort(jax.random.randint(keys[6], (block_count, SLOTS), 0, 1 << 20), axis=1, stable=True)
    placed = jnp.take_along_axis(chosen, shuffle, axis=1)
    return placed.reshape(N_TM, N_CLIPS * SLOTS, 1).astype(jnp.int32)


def scatter_about(rng, shape, scale, limit, kind=jnp.bfloat16):
    return jnp.clip(scale * jax.random.normal(rng, shape, jnp.float32), -limit, limit).astype(kind)


def setup_inputs(seed: int = 0, part: int = 0) -> dict:
    key_list = jax.random.split(jax.random.key(seed), 5)
    own_keys = jax.random.split(jax.random.fold_in(key_list[4], part), 5)
    return {
        "video": draw_video(jax.random.fold_in(jax.random.fold_in(key_list[4], part), 71), part),
        "frame_owner": draw_frame_owner(jax.random.fold_in(jax.random.fold_in(key_list[4], part), 71), part),
        "conv_first": scatter_about(key_list[2], (KT, KS, KS, C, C), (KT * KS * KS * C) ** -0.5, 0.109375),
        "conv_second": scatter_about(key_list[3], (KT, KS, KS, C, C), (KT * KS * KS * C) ** -0.5, 0.109375),
    }


EPSILON = 1e-06

def normalize(values):
    values = values.astype(jnp.float32)
    meansq = lax.optimization_barrier(jnp.mean(values * values, axis=-1, keepdims=True))
    return jax.nn.silu(values * lax.rsqrt(meansq + EPSILON))

def delayed(values, lag_rows, keep_mask):
    shifted = jnp.concatenate([jnp.zeros_like(values[:lag_rows]), values[:-lag_rows]], axis=0)
    return jnp.where(keep_mask[:, None, None, None], shifted, jnp.zeros_like(shifted))

def causal_conv(current, earlier, earliest, weights):
    stacked = jnp.concatenate([current, earlier, earliest], axis=-1).astype(jnp.float32)
    kernel = jnp.concatenate([weights[0], weights[1], weights[2]], axis=2).astype(jnp.float32)
    return lax.conv_general_dilated(stacked, kernel, (1, 1), 'SAME', dimension_numbers=('NHWC', 'HWIO', 'NHWC'))

def reference(video, frame_owner, conv_first, conv_second):
    rows_all = N_TM * N_CLIPS * SLOTS
    owners = frame_owner.reshape(rows_all).astype(jnp.int32)
    flat_video = video.reshape(rows_all, TILE_H, TILE_W, C)
    sequence = jnp.argsort(owners, stable=True).astype(jnp.int32)
    sorted_owner = owners[sequence]
    frames = flat_video[sequence]
    same_one = jnp.concatenate([jnp.zeros((1,), jnp.bool_), sorted_owner[1:] == sorted_owner[:-1]])
    same_two = jnp.concatenate([jnp.zeros((2,), jnp.bool_), sorted_owner[2:] == sorted_owner[:-2]])
    active = normalize(frames).astype(jnp.bfloat16)
    hidden = causal_conv(active, delayed(active, 1, same_one), delayed(active, 2, same_two), conv_first).astype(jnp.bfloat16)
    second = normalize(hidden).astype(jnp.bfloat16)
    update = causal_conv(second, delayed(second, 1, same_one), delayed(second, 2, same_two), conv_second)
    result = (frames.astype(jnp.float32) + update).astype(jnp.bfloat16)
    blocks = owners.reshape(N_TM * N_CLIPS, SLOTS)
    onehot = (blocks[:, :, None] == jnp.arange(N_CLIPS, dtype=jnp.int32)[None, None, :]).astype(jnp.int32)
    rank_table = jnp.cumsum(onehot, axis=1) - 1
    slot_rank = lax.optimization_barrier(jnp.sum(rank_table * onehot, axis=2)).reshape(rows_all)
    row_ids = jnp.arange(rows_all, dtype=jnp.int32)
    period = row_ids // (N_CLIPS * SLOTS)
    reader = row_ids // SLOTS % N_CLIPS
    target = period * (N_CLIPS * N_CLIPS * CAP) + owners * (N_CLIPS * CAP) + reader * CAP + slot_rank
    placed = jnp.zeros((N_TM * N_CLIPS * N_CLIPS * CAP, TILE_H, TILE_W, C), result.dtype)
    placed = placed.at[target[sequence]].set(result)
    return placed.reshape(N_TM, N_CLIPS * N_CLIPS * CAP, TILE_H, TILE_W, C)
```

```python
import functools

import jax
import jax.numpy as jnp
from jax import lax
from jax.experimental import pallas as pl
from jax.experimental.pallas import tpu as pltpu
from jax.sharding import PartitionSpec as P

EPSILON = 1e-06
MESH = pl.DeviceIdType.MESH
HALO = 4


def each(count, step):
    if count <= 8:
        for i in range(count):
            step(i)
    else:
        lax.fori_loop(0, count, lambda i, c: (step(i), c)[1], 0)


def exchange_kernel(
    sizes, video, owners, own, halo, counts,
    raw, packed, outbox, tailbox, count_row, after, before,
    load_sem, send_sem, tail_send, count_send, recv_sem, count_recv, pass_send, pass_recv,
):
    readers, periods, slots, cap, depth = sizes
    g = lax.axis_index("groups")
    r = lax.axis_index("clips")
    p = lax.axis_index("tm")
    c = lax.axis_index("chan")
    load = pltpu.make_async_copy(video.at[0], raw, load_sem)
    load.start()

    barrier = pltpu.get_barrier_semaphore()

    def greet(i):
        dp, dr = i // readers, i % readers
        pp, rr = lax.rem(p + dp, periods), lax.rem(r + dr, readers)

        @pl.when(i > 0)
        def _():
            pl.semaphore_signal(barrier, inc=1, device_id=(g, rr, pp, c), device_id_type=MESH)

    each(periods * readers, greet)
    pl.semaphore_signal(barrier, inc=1, device_id=(g, r, p, 1 - c), device_id_type=MESH)

    lane = lax.broadcasted_iota(jnp.int32, (1, 128), 1)
    tally = jnp.zeros((1, 128), jnp.int32)
    names = [owners[0, s] for s in range(slots)]
    for s in range(slots):
        tally = tally + jnp.where(lane == names[s], 1, 0)
    count_row[...] = tally
    counts[p * readers + r] = tally

    def tables(o):
        base = o * 32
        n = jnp.int32(slots)
        after[base + slots] = n
        after[base + slots + 1] = n
        for s in reversed(range(slots)):
            n = jnp.where(names[s] == o, s, n)
            after[base + s] = n
        m = jnp.int32(-1)
        before[base] = m
        for s in range(slots):
            m = jnp.where(names[s] == o, s, m)
            before[base + s + 1] = m

    each(readers, tables)

    load.wait()
    for s in range(slots):
        v = raw[s].astype(jnp.float32).reshape(32, 64)
        packed[s] = jnp.concatenate([v[:16], v[16:]], axis=1).astype(jnp.bfloat16)

    def pack(i):
        o = lax.rem(r + i, readers)
        s = after[o * 32]
        for k in range(cap):
            outbox[i, k] = packed[jnp.minimum(s, slots - 1)]
            s = after[o * 32 + s + 1]
        m = before[o * 32 + slots]
        for k in range(depth):
            m = jnp.maximum(m, 0)
            tailbox[i, k] = packed[m]
            m = before[o * 32 + m]

    each(readers, pack)
    mine = pl.ds(r * cap, cap)
    for k in range(cap):
        own[c, r * cap + k] = outbox[0, k]
    pl.semaphore_wait(barrier, periods * readers)

    source = p * readers + r

    def send_own(i):
        o = lax.rem(r + i, readers)
        to = (g, o, p, c)
        return (
            pltpu.make_async_remote_copy(
                outbox.at[i], own.at[c, mine], send_sem.at[i], recv_sem.at[source],
                device_id=to, device_id_type=MESH),
            pltpu.make_async_remote_copy(
                count_row, counts.at[source], count_send.at[i], count_recv.at[source],
                device_id=to, device_id_type=MESH),
        )

    def send_tail(j):
        dp, i = 1 + j // readers, j % readers
        to = (g, lax.rem(r + i, readers), p + dp, c)
        return (
            pltpu.make_async_remote_copy(
                tailbox.at[i], halo.at[c, pl.ds(source * depth, depth)],
                tail_send.at[j], recv_sem.at[source], device_id=to, device_id_type=MESH),
            pltpu.make_async_remote_copy(
                count_row, counts.at[source], count_send.at[readers + j], count_recv.at[source],
                device_id=to, device_id_type=MESH),
        )

    def start_own(i):
        for d in send_own(i + 1):
            d.start()

    def start_tail(j):
        @pl.when(p + 1 + j // readers < periods)
        def _():
            for d in send_tail(j):
                d.start()

    each(readers - 1, start_own)
    each((periods - 1) * readers, start_tail)

    def relay_own(rr):
        part = own.at[c, pl.ds(rr * cap, cap)]
        q = p * readers + rr
        return pltpu.make_async_remote_copy(
            part, part, pass_send.at[q], pass_recv.at[q],
            device_id=(g, r, p, 1 - c), device_id_type=MESH)

    def relay_tail(q):
        part = halo.at[c, pl.ds(q * depth, depth)]
        return pltpu.make_async_remote_copy(
            part, part, pass_send.at[q], pass_recv.at[q],
            device_id=(g, r, p, 1 - c), device_id_type=MESH)

    relay_own(r).start()

    def arrive_own(i):
        rr = lax.rem(r + i + 1, readers)
        q = p * readers + rr
        part = own.at[c, pl.ds(rr * cap, cap)]
        pltpu.make_async_remote_copy(
            part, part, send_sem.at[0], recv_sem.at[q],
            device_id=(g, rr, p, c), device_id_type=MESH).wait_recv()
        relay_own(rr).start()

    def arrive_tail(q):
        @pl.when(q < p * readers)
        def _():
            part = halo.at[c, pl.ds(q * depth, depth)]
            pltpu.make_async_remote_copy(
                part, part, send_sem.at[0], recv_sem.at[q],
                device_id=(g, lax.rem(q, readers), 0, c), device_id_type=MESH).wait_recv()
            relay_tail(q).start()

    each(readers - 1, arrive_own)
    each((periods - 1) * readers, arrive_tail)

    def count_wait(q):
        pltpu.make_async_remote_copy(
            count_row, counts.at[q], count_send.at[0], count_recv.at[q],
            device_id=(g, r, p, 1 - c), device_id_type=MESH).wait_recv()

    def finish_own(i):
        for d in send_own(i + 1):
            d.wait_send()
        count_wait(p * readers + lax.rem(r + i + 1, readers))

    def finish_tail(j):
        @pl.when(p + 1 + j // readers < periods)
        def _():
            for d in send_tail(j):
                d.wait_send()

    def finish_halo(q):
        @pl.when(q < p * readers)
        def _():
            count_wait(q)
            relay_tail(q).wait_send()
            part = halo.at[1 - c, pl.ds(q * depth, depth)]
            pltpu.make_async_remote_copy(
                part, part, pass_send.at[q], pass_recv.at[q],
                device_id=(g, r, p, 1 - c), device_id_type=MESH).wait_recv()

    def finish_relay(rr):
        q = p * readers + rr
        relay_own(rr).wait_send()
        part = own.at[1 - c, pl.ds(rr * cap, cap)]
        pltpu.make_async_remote_copy(
            part, part, pass_send.at[q], pass_recv.at[q],
            device_id=(g, r, p, 1 - c), device_id_type=MESH).wait_recv()

    each(readers - 1, finish_own)
    each((periods - 1) * readers, finish_tail)
    each((periods - 1) * readers, finish_halo)
    each(readers, finish_relay)


def normalize(values):
    meansq = jnp.mean(values * values, axis=-1, keepdims=True)
    v = values * lax.rsqrt(meansq + EPSILON)
    return v / (1.0 + jnp.exp(-v))


def spread(values, target, first, frames):
    x = values.reshape(frames * 4, 8, 128)
    column = lax.broadcasted_iota(jnp.int32, (1, 8, 128), 1)
    shifted = [
        jnp.where(column == 0, 0.0, pltpu.roll(x, 1, 1)),
        x,
        jnp.where(column == 7, 0.0, pltpu.roll(x, 7, 1)),
    ]
    blank = jnp.zeros((frames, 1, 8, 128), jnp.float32)
    rows = pl.ds(first * 32, frames * 32)
    for v in range(3):
        y = shifted[v].reshape(frames, 4, 8, 128)
        lines = [
            jnp.concatenate([blank, y[:, :3]], axis=1),
            y,
            jnp.concatenate([y[:, 1:], blank], axis=1),
        ]
        for u in range(3):
            tap = u * 3 + v
            target[rows, tap * 128 : (tap + 1) * 128] = (
                lines[u].reshape(frames * 32, 128).astype(jnp.bfloat16)
            )


def conv_kernel(sizes, counts, own, halo, first, second, out, x0, taps_a, taps_b, total):
    readers, periods, slots, cap, depth = sizes
    o = lax.axis_index("clips")
    p = lax.axis_index("tm")
    c = lax.axis_index("chan")
    frames = readers * cap

    number = [counts[p * readers + q, 0, o] for q in range(readers)]
    base = [jnp.int32(0)]
    for q in range(readers):
        base.append(base[-1] + number[q])
    live = base[readers]

    def join(a, b, valid):
        a = a.astype(jnp.float32)
        b = b.astype(jnp.float32)
        whole = jnp.concatenate(
            [
                jnp.concatenate([a[:, :64], b[:, :64]], axis=1),
                jnp.concatenate([a[:, 64:], b[:, 64:]], axis=1),
            ],
            axis=0,
        )
        return jnp.where(valid, whole, 0.0)

    where_tail = [jnp.int32(0)] * HALO
    has_tail = [jnp.bool_(False)] * HALO
    seen = jnp.int32(0)
    for q in reversed(range((periods - 1) * readers)):
        n = jnp.where(q < p * readers, counts[q, 0, o], 0)
        for m in range(HALO):
            hit = (seen <= m) & (m < seen + n)
            where_tail[m] = jnp.where(hit, q * depth + m - seen, where_tail[m])
            has_tail[m] = has_tail[m] | hit
        seen = seen + n
    for m in range(HALO):
        at = where_tail[m]
        x0[HALO - 1 - m] = join(halo[0, at], halo[1, at], has_tail[m])
    for j in range(frames):
        at = jnp.int32(j)
        for q in range(1, readers):
            at = jnp.where(j >= base[q], q * cap + j - base[q], at)
        at = jnp.minimum(at, frames - 1)
        x0[HALO + j] = join(own[0, at], own[1, at], j < live)

    def blocks(count, lead):
        yield 0, lead
        for b in range(lead, count, 8):
            yield b, min(8, count - b)

    for at, n in blocks(frames + HALO, HALO):
        spread(normalize(x0[at : at + n].reshape(n * 32, 128)), taps_a, at, n)

    def conv(taps, weights, at, n):
        acc = None
        for t in range(3):
            rows = pl.ds((at + 2 - t) * 32, n * 32)
            part = jnp.dot(taps[rows, :], weights[t], preferred_element_type=jnp.float32)
            acc = part if acc is None else acc + part
        return acc

    for at, n in blocks(frames + 2, 2):
        hidden = conv(taps_a, first, at, n).astype(jnp.bfloat16).astype(jnp.float32)
        spread(normalize(hidden), taps_b, at, n)

    for at in range(0, frames, 8):
        update = conv(taps_b, second, at, 8)
        y = x0[HALO + at : HALO + at + 8].reshape(256, 128) + update
        y = jnp.where(c == 0, y[:, :64], y[:, 64:])
        total[at : at + 8] = y.reshape(8, 32, 64)

    for q in range(readers):
        for k in range(cap):
            y = total[jnp.minimum(base[q] + k, frames - 1)]
            y = jnp.where(k < number[q], y, 0.0)
            out[0, q * cap + k] = y.reshape(4, 8, 64).astype(jnp.bfloat16)


def body(video, frame_owner, conv_first, conv_second):
    readers = lax.axis_size("clips")
    periods = lax.axis_size("tm")
    slots = video.shape[1]
    cap = max(2, 2 * slots // readers)
    depth = min(HALO, cap)
    frames = readers * cap
    sizes = (readers, periods, slots, cap, depth)
    sources = periods * readers
    vmem = pl.BlockSpec(memory_space=pltpu.VMEM)
    smem = pl.BlockSpec(memory_space=pltpu.SMEM)
    anywhere = pl.BlockSpec(memory_space=pl.ANY)
    dma = pltpu.SemaphoreType.DMA
    own, halo, counts = pl.pallas_call(
        functools.partial(exchange_kernel, sizes),
        out_shape=(
            jax.ShapeDtypeStruct((2, frames, 16, 128), jnp.bfloat16),
            jax.ShapeDtypeStruct((2, (periods - 1) * readers * depth, 16, 128), jnp.bfloat16),
            jax.ShapeDtypeStruct((sources, 1, 128), jnp.int32),
        ),
        in_specs=[anywhere, smem],
        out_specs=(vmem, vmem, vmem),
        scratch_shapes=[
            pltpu.VMEM((slots, 4, 8, 64), jnp.bfloat16),
            pltpu.VMEM((slots, 16, 128), jnp.bfloat16),
            pltpu.VMEM((readers, cap, 16, 128), jnp.bfloat16),
            pltpu.VMEM((readers, depth, 16, 128), jnp.bfloat16),
            pltpu.VMEM((1, 128), jnp.int32),
            pltpu.SMEM((readers * 32,), jnp.int32),
            pltpu.SMEM((readers * 32,), jnp.int32),
            dma,
            dma((readers,)),
            dma((sources,)),
            dma((sources,)),
            dma((sources,)),
            dma((sources,)),
            dma((sources,)),
            dma((sources,)),
        ],
        compiler_params=pltpu.CompilerParams(
            collective_id=0, has_side_effects=True, vmem_limit_bytes=24 * 2**20
        ),
    )(video, frame_owner.reshape(1, slots))

    return pl.pallas_call(
        functools.partial(conv_kernel, sizes),
        out_shape=jax.ShapeDtypeStruct((1, frames, 4, 8, 64), jnp.bfloat16),
        in_specs=[smem, vmem, vmem, vmem, vmem],
        out_specs=vmem,
        scratch_shapes=[
            pltpu.VMEM((frames + HALO, 32, 128), jnp.float32),
            pltpu.VMEM(((frames + HALO) * 32, 1152), jnp.bfloat16),
            pltpu.VMEM(((frames + 2) * 32, 1152), jnp.bfloat16),
            pltpu.VMEM((frames, 32, 64), jnp.float32),
        ],
        compiler_params=pltpu.CompilerParams(vmem_limit_bytes=32 * 2**20),
    )(counts, own, halo, conv_first.reshape(3, 1152, 128), conv_second.reshape(3, 1152, 128))


def solution(mesh):
    placed = (
        P(("groups", "tm"), "clips", None, None, "chan"),
        P(("groups", "tm"), "clips", None),
        P(),
        P(),
    )
    return jax.shard_map(
        body,
        mesh=mesh,
        in_specs=placed,
        out_specs=P(("groups", "tm"), "clips", None, None, "chan"),
        check_vma=False,
    )
```

```python
import functools

import jax
import jax.numpy as jnp
from jax import lax
from jax.experimental import pallas as pl
from jax.experimental.pallas import tpu as pltpu
from jax.sharding import PartitionSpec as P

EPSILON = 1e-06
MESH = pl.DeviceIdType.MESH
HALO = 4


def each(count, step):
    if count <= 8:
        for i in range(count):
            step(i)
    else:
        lax.fori_loop(0, count, lambda i, c: (step(i), c)[1], 0)


def block_kernel(
    sizes, video, owner_rows, first_in, second_in, out,
    own, halo, counts, first, second, known, x0, taps_a, taps_b, total,
    owners, raw, packed, outbox, tailbox, count_row, after, before,
    known_sem, load_sem, owner_sem, weight_sem, send_sem, tail_send, count_send, recv_sem, count_recv, pass_send, pass_recv,
):
    readers, periods, slots, cap, depth = sizes
    g = lax.axis_index("groups")
    r = lax.axis_index("clips")
    p = lax.axis_index("tm")
    c = lax.axis_index("chan")
    load = pltpu.make_async_copy(video.at[0], raw, load_sem)
    name_load = pltpu.make_async_copy(owner_rows, owners, owner_sem)
    name_load.start()
    load.start()
    weight_loads = [
        pltpu.make_async_copy(first_in, first, weight_sem.at[0]),
        pltpu.make_async_copy(second_in, second, weight_sem.at[1]),
    ]

    barrier = pltpu.get_barrier_semaphore()

    def greet(i):
        dp, dr = i // readers, i % readers
        pp, rr = lax.rem(p + dp, periods), lax.rem(r + dr, readers)

        @pl.when(i > 0)
        def _():
            pl.semaphore_signal(barrier, inc=1, device_id=(g, rr, pp, c), device_id_type=MESH)

    each(periods * readers, greet)
    pl.semaphore_signal(barrier, inc=1, device_id=(g, r, p, 1 - c), device_id_type=MESH)

    for d in weight_loads:
        d.start()
    name_load.wait()
    lane = lax.broadcasted_iota(jnp.int32, (1, 128), 1)
    tally = jnp.zeros((1, 128), jnp.int32)
    names = [owners[0, s] for s in range(slots)]
    for s in range(slots):
        tally = tally + jnp.where(lane == names[s], 1, 0)
    count_row[...] = tally
    counts[p * readers + r] = tally

    def tables(o):
        base = o * 32
        n = jnp.int32(slots)
        after[base + slots] = n
        after[base + slots + 1] = n
        for s in reversed(range(slots)):
            n = jnp.where(names[s] == o, s, n)
            after[base + s] = n
        m = jnp.int32(-1)
        before[base] = m
        for s in range(slots):
            m = jnp.where(names[s] == o, s, m)
            before[base + s + 1] = m

    each(readers, tables)

    load.wait()
    for s in range(slots):
        v = raw[s].astype(jnp.float32).reshape(32, 64)
        packed[s] = jnp.concatenate([v[:16], v[16:]], axis=1).astype(jnp.bfloat16)

    def pack(i):
        o = lax.rem(r + i, readers)
        s = after[o * 32]
        for k in range(cap):
            outbox[i, k] = packed[jnp.minimum(s, slots - 1)]
            s = after[o * 32 + s + 1]
        m = before[o * 32 + slots]
        for k in range(depth):
            m = jnp.maximum(m, 0)
            tailbox[i, k] = packed[m]
            m = before[o * 32 + m]

    each(readers, pack)
    mine = pl.ds(r * cap, cap)
    for k in range(cap):
        own[c, r * cap + k] = outbox[0, k]
    pl.semaphore_wait(barrier, periods * readers)

    source = p * readers + r

    def send_own(i):
        o = lax.rem(r + i, readers)
        to = (g, o, p, c)
        return (
            pltpu.make_async_remote_copy(
                outbox.at[i], own.at[c, mine], send_sem.at[i], recv_sem.at[source],
                device_id=to, device_id_type=MESH),
            pltpu.make_async_remote_copy(
                count_row, counts.at[source], count_send.at[i], count_recv.at[source],
                device_id=to, device_id_type=MESH),
        )

    def send_tail(j):
        dp, i = 1 + j // readers, j % readers
        to = (g, lax.rem(r + i, readers), p + dp, c)
        return (
            pltpu.make_async_remote_copy(
                tailbox.at[i], halo.at[c, pl.ds(source * depth, depth)],
                tail_send.at[j], recv_sem.at[source], device_id=to, device_id_type=MESH),
            pltpu.make_async_remote_copy(
                count_row, counts.at[source], count_send.at[readers + j], count_recv.at[source],
                device_id=to, device_id_type=MESH),
        )

    def start_own(i):
        for d in send_own(i + 1):
            d.start()

    def start_tail(j):
        @pl.when(p + 1 + j // readers < periods)
        def _():
            for d in send_tail(j):
                d.start()

    each(readers - 1, start_own)
    each((periods - 1) * readers, start_tail)

    def relay_own(rr):
        part = own.at[c, pl.ds(rr * cap, cap)]
        q = p * readers + rr
        return pltpu.make_async_remote_copy(
            part, part, pass_send.at[q], pass_recv.at[q],
            device_id=(g, r, p, 1 - c), device_id_type=MESH)

    def relay_tail(q):
        part = halo.at[c, pl.ds(q * depth, depth)]
        return pltpu.make_async_remote_copy(
            part, part, pass_send.at[q], pass_recv.at[q],
            device_id=(g, r, p, 1 - c), device_id_type=MESH)

    relay_own(r).start()

    def count_wait(q):
        pltpu.make_async_remote_copy(
            count_row, counts.at[q], count_send.at[0], count_recv.at[q],
            device_id=(g, r, p, 1 - c), device_id_type=MESH).wait_recv()

    def count_own(i):
        count_wait(p * readers + lax.rem(r + i + 1, readers))

    def count_tail(q):
        @pl.when(q < p * readers)
        def _():
            count_wait(q)

    each(readers - 1, count_own)
    each((periods - 1) * readers, count_tail)
    known_copy = pltpu.make_async_copy(counts, known, known_sem)
    known_copy.start()

    def arrive_own(i):
        rr = lax.rem(r + i + 1, readers)
        q = p * readers + rr
        part = own.at[c, pl.ds(rr * cap, cap)]
        pltpu.make_async_remote_copy(
            part, part, send_sem.at[0], recv_sem.at[q],
            device_id=(g, rr, p, c), device_id_type=MESH).wait_recv()
        relay_own(rr).start()

    def arrive_tail(q):
        @pl.when(q < p * readers)
        def _():
            part = halo.at[c, pl.ds(q * depth, depth)]
            pltpu.make_async_remote_copy(
                part, part, send_sem.at[0], recv_sem.at[q],
                device_id=(g, lax.rem(q, readers), 0, c), device_id_type=MESH).wait_recv()
            relay_tail(q).start()

    each(readers - 1, arrive_own)
    each((periods - 1) * readers, arrive_tail)

    def finish_own(i):
        for d in send_own(i + 1):
            d.wait_send()

    def finish_tail(j):
        @pl.when(p + 1 + j // readers < periods)
        def _():
            for d in send_tail(j):
                d.wait_send()

    def finish_halo(q):
        @pl.when(q < p * readers)
        def _():
            relay_tail(q).wait_send()

    def get_halo(q):
        @pl.when(q < p * readers)
        def _():
            part = halo.at[1 - c, pl.ds(q * depth, depth)]
            pltpu.make_async_remote_copy(
                part, part, pass_send.at[q], pass_recv.at[q],
                device_id=(g, r, p, 1 - c), device_id_type=MESH).wait_recv()

    def finish_relay(rr):
        relay_own(rr).wait_send()

    def get_relay(rr):
        q = p * readers + rr
        part = own.at[1 - c, pl.ds(rr * cap, cap)]
        pltpu.make_async_remote_copy(
            part, part, pass_send.at[q], pass_recv.at[q],
            device_id=(g, r, p, 1 - c), device_id_type=MESH).wait_recv()

    each((periods - 1) * readers, get_halo)
    each(readers, get_relay)
    known_copy.wait()
    weight_loads[0].wait()
    convolve(sizes, known, own, halo, first, second, weight_loads[1], out, x0, taps_a, taps_b, total)
    each(readers - 1, finish_own)
    each((periods - 1) * readers, finish_tail)
    each((periods - 1) * readers, finish_halo)
    each(readers, finish_relay)


def normalize(values):
    meansq = jnp.mean(values * values, axis=-1, keepdims=True)
    v = values * lax.rsqrt(meansq + EPSILON)
    return v / (1.0 + jnp.exp(-v))


def spread(values, target, first, frames):
    x = values.reshape(frames * 4, 8, 128)
    column = lax.broadcasted_iota(jnp.int32, (1, 8, 128), 1)
    shifted = [
        jnp.where(column == 0, 0.0, pltpu.roll(x, 1, 1)),
        x,
        jnp.where(column == 7, 0.0, pltpu.roll(x, 7, 1)),
    ]
    blank = jnp.zeros((frames, 1, 8, 128), jnp.float32)
    rows = pl.ds(first * 32, frames * 32)
    for v in range(3):
        y = shifted[v].reshape(frames, 4, 8, 128)
        lines = [
            jnp.concatenate([blank, y[:, :3]], axis=1),
            y,
            jnp.concatenate([y[:, 1:], blank], axis=1),
        ]
        for u in range(3):
            tap = u * 3 + v
            target[rows, tap * 128 : (tap + 1) * 128] = (
                lines[u].reshape(frames * 32, 128).astype(jnp.bfloat16)
            )


def convolve(sizes, counts, own, halo, first, second, second_load, out, x0, taps_a, taps_b, total):
    readers, periods, slots, cap, depth = sizes
    o = lax.axis_index("clips")
    p = lax.axis_index("tm")
    c = lax.axis_index("chan")
    frames = readers * cap

    number = [counts[p * readers + q, 0, o] for q in range(readers)]
    base = [jnp.int32(0)]
    for q in range(readers):
        base.append(base[-1] + number[q])
    live = base[readers]

    def join(a, b, valid):
        a = a.astype(jnp.float32)
        b = b.astype(jnp.float32)
        whole = jnp.concatenate(
            [
                jnp.concatenate([a[:, :64], b[:, :64]], axis=1),
                jnp.concatenate([a[:, 64:], b[:, 64:]], axis=1),
            ],
            axis=0,
        )
        return jnp.where(valid, whole, 0.0)

    where_tail = [jnp.int32(0)] * HALO
    has_tail = [jnp.bool_(False)] * HALO
    seen = jnp.int32(0)
    for q in reversed(range((periods - 1) * readers)):
        n = jnp.where(q < p * readers, counts[q, 0, o], 0)
        for m in range(HALO):
            hit = (seen <= m) & (m < seen + n)
            where_tail[m] = jnp.where(hit, q * depth + m - seen, where_tail[m])
            has_tail[m] = has_tail[m] | hit
        seen = seen + n
    for m in range(HALO):
        at = where_tail[m]
        x0[HALO - 1 - m] = join(halo[0, at], halo[1, at], has_tail[m])
    for j in range(frames):
        at = jnp.int32(j)
        for q in range(1, readers):
            at = jnp.where(j >= base[q], q * cap + j - base[q], at)
        at = jnp.minimum(at, frames - 1)
        x0[HALO + j] = join(own[0, at], own[1, at], j < live)

    def blocks(count, lead):
        yield 0, lead
        for b in range(lead, count, 8):
            yield b, min(8, count - b)

    for at, n in blocks(frames + HALO, HALO):
        spread(normalize(x0[at : at + n].reshape(n * 32, 128)), taps_a, at, n)

    def conv(taps, weights, at, n):
        acc = None
        for t in range(3):
            rows = pl.ds((at + 2 - t) * 32, n * 32)
            part = jnp.dot(taps[rows, :], weights[t], preferred_element_type=jnp.float32)
            acc = part if acc is None else acc + part
        return acc

    for at, n in blocks(frames + 2, 2):
        hidden = conv(taps_a, first, at, n).astype(jnp.bfloat16).astype(jnp.float32)
        spread(normalize(hidden), taps_b, at, n)

    second_load.wait()
    for at in range(0, frames, 8):
        update = conv(taps_b, second, at, 8)
        y = x0[HALO + at : HALO + at + 8].reshape(256, 128) + update
        y = jnp.where(c == 0, y[:, :64], y[:, 64:])
        total[at : at + 8] = y.reshape(8, 32, 64)

    for q in range(readers):
        for k in range(cap):
            y = total[jnp.minimum(base[q] + k, frames - 1)]
            y = jnp.where(k < number[q], y, 0.0)
            out[0, q * cap + k] = y.reshape(4, 8, 64).astype(jnp.bfloat16)


def body(video, frame_owner, conv_first, conv_second):
    readers = lax.axis_size("clips")
    periods = lax.axis_size("tm")
    slots = video.shape[1]
    cap = max(2, 2 * slots // readers)
    depth = min(HALO, cap)
    frames = readers * cap
    sizes = (readers, periods, slots, cap, depth)
    sources = periods * readers
    vmem = pl.BlockSpec(memory_space=pltpu.VMEM)
    hbm = pl.BlockSpec(memory_space=pltpu.HBM)
    dma = pltpu.SemaphoreType.DMA
    return pl.pallas_call(
        functools.partial(block_kernel, sizes),
        out_shape=jax.ShapeDtypeStruct((1, frames, 4, 8, 64), jnp.bfloat16),
        in_specs=[hbm] * 4,
        out_specs=vmem,
        scratch_shapes=[
            pltpu.VMEM((2, frames, 16, 128), jnp.bfloat16),
            pltpu.VMEM((2, (periods - 1) * readers * depth, 16, 128), jnp.bfloat16),
            pltpu.VMEM((sources, 1, 128), jnp.int32),
            pltpu.VMEM((3, 1152, 128), jnp.bfloat16),
            pltpu.VMEM((3, 1152, 128), jnp.bfloat16),
            pltpu.SMEM((sources, 1, 128), jnp.int32),
            pltpu.VMEM((frames + HALO, 32, 128), jnp.float32),
            pltpu.VMEM(((frames + HALO) * 32, 1152), jnp.bfloat16),
            pltpu.VMEM(((frames + 2) * 32, 1152), jnp.bfloat16),
            pltpu.VMEM((frames, 32, 64), jnp.float32),
            pltpu.SMEM((1, slots), jnp.int32),
            pltpu.VMEM((slots, 4, 8, 64), jnp.bfloat16),
            pltpu.VMEM((slots, 16, 128), jnp.bfloat16),
            pltpu.VMEM((readers, cap, 16, 128), jnp.bfloat16),
            pltpu.VMEM((readers, depth, 16, 128), jnp.bfloat16),
            pltpu.VMEM((1, 128), jnp.int32),
            pltpu.SMEM((readers * 32,), jnp.int32),
            pltpu.SMEM((readers * 32,), jnp.int32),
            dma,
            dma,
            dma,
            dma((2,)),
            dma((readers,)),
            dma((sources,)),
            dma((sources,)),
            dma((sources,)),
            dma((sources,)),
            dma((sources,)),
            dma((sources,)),
        ],
        compiler_params=pltpu.CompilerParams(
            collective_id=0, has_side_effects=True, vmem_limit_bytes=60 * 2**20
        ),
    )(
        video,
        frame_owner.reshape(1, slots),
        conv_first.reshape(3, 1152, 128),
        conv_second.reshape(3, 1152, 128),
    )


def solution(mesh):
    placed = (
        P(("groups", "tm"), "clips", None, None, "chan"),
        P(("groups", "tm"), "clips", None),
        P(),
        P(),
    )
    return jax.shard_map(
        body,
        mesh=mesh,
        in_specs=placed,
        out_specs=P(("groups", "tm"), "clips", None, None, "chan"),
        check_vma=False,
    )
```

```python
import functools

import jax
import jax.numpy as jnp
from jax import lax
from jax.experimental import pallas as pl
from jax.experimental.pallas import tpu as pltpu
from jax.sharding import PartitionSpec as P

EPSILON = 1e-06
MESH = pl.DeviceIdType.MESH
HALO = 4


def each(count, step):
    if count <= 8:
        for i in range(count):
            step(i)
    else:
        lax.fori_loop(0, count, lambda i, c: (step(i), c)[1], 0)


def block_kernel(
    sizes, video, owner_rows, first_in, second_in, out,
    box, other, tail_in, tail_out, counts, known, first, second, x0, taps_a, taps_b, total,
    owners, raw, packed, after,
    known_sem, load_sem, owner_sem, weight_sem, send_sem, recv_sem, count_send, count_recv,
    pass_send, pass_recv, tail_send, tail_recv,
):
    readers, periods, slots, cap = sizes
    frames = readers * cap
    g = lax.axis_index("groups")
    r = lax.axis_index("clips")
    p = lax.axis_index("tm")
    c = lax.axis_index("chan")
    load = pltpu.make_async_copy(video.at[0], raw, load_sem)
    name_load = pltpu.make_async_copy(owner_rows, owners, owner_sem)
    name_load.start()
    load.start()
    weight_loads = [
        pltpu.make_async_copy(first_in, first, weight_sem.at[0]),
        pltpu.make_async_copy(second_in, second, weight_sem.at[1]),
    ]
    up = (g, r + 1, p, c)
    down = (g, r - 1, p, c)
    later = (g, r, p + 1, c)
    earlier = (g, r, p - 1, c)
    sibling = (g, r, p, 1 - c)

    barrier = pltpu.get_barrier_semaphore()

    def greet(there, who):
        @pl.when(there)
        def _():
            pl.semaphore_signal(barrier, inc=1, device_id=who, device_id_type=MESH)

    greet(r < readers - 1, up)
    greet(r > 0, down)
    greet(p < periods - 1, later)
    greet(p > 0, earlier)
    pl.semaphore_signal(barrier, inc=1, device_id=sibling, device_id_type=MESH)
    for d in weight_loads:
        d.start()

    name_load.wait()
    lane = lax.broadcasted_iota(jnp.int32, (1, 128), 1)
    tally = jnp.zeros((1, 128), jnp.int32)
    names = [owners[0, s] for s in range(slots)]
    for s in range(slots):
        tally = tally + jnp.where(lane == names[s], 1, 0)
    counts[r] = tally

    def tables(o):
        base = o * 32
        n = jnp.int32(slots)
        after[base + slots] = n
        after[base + slots + 1] = n
        for s in reversed(range(slots)):
            n = jnp.where(names[s] == o, s, n)
            after[base + s] = n

    each(readers, tables)

    load.wait()
    for s in range(slots):
        v = raw[s].astype(jnp.float32).reshape(32, 64)
        packed[s] = jnp.concatenate([v[:16], v[16:]], axis=1).astype(jnp.bfloat16)

    def pack(o):
        s = after[o * 32]
        for k in range(cap):
            box[r, o, k] = packed[jnp.minimum(s, slots - 1)]
            s = after[o * 32 + s + 1]

    each(readers, pack)
    neighbours = (
        1
        + jnp.where(r < readers - 1, 1, 0)
        + jnp.where(r > 0, 1, 0)
        + jnp.where(p < periods - 1, 1, 0)
        + jnp.where(p > 0, 1, 0)
    )
    pl.semaphore_wait(barrier, neighbours)

    def remote(source, target, sent, got, who):
        return pltpu.make_async_remote_copy(
            source, target, sent, got, device_id=who, device_id_type=MESH)

    def chunk(s, d, who):
        at = s * readers + d
        return remote(box.at[s, d], box.at[s, d], send_sem.at[at], recv_sem.at[at], who)

    def row(s, way, who):
        return remote(
            counts.at[s], counts.at[s], count_send.at[2 * s + way], count_recv.at[s], who)

    def relay(s):
        return remote(box.at[s, r], other.at[s], pass_send.at[s], pass_recv.at[s], sibling)

    def when(there, act):
        @pl.when(there)
        def _():
            act()

    def start_rows():
        when(r < readers - 1, lambda: row(r, 0, up).start())
        when(r > 0, lambda: row(r, 1, down).start())

    def start_chunks(i):
        d = readers - 1 - i
        when(d > r, lambda: chunk(r, d, up).start())
        when(i < r, lambda: chunk(r, i, down).start())

    each(readers, start_chunks)
    start_rows()
    relay(r).start()

    def arrive(i):
        below, above = r - 1 - i, r + 1 + i

        def from_below(j):
            d = readers - 1 - j

            def take():
                chunk(below, d, up).wait_recv()
                when(d > r, lambda: chunk(below, d, up).start())
                when(d == r, lambda: relay(below).start())

            when((below >= 0) & (d >= r), take)

        def from_above(d):
            def take():
                chunk(above, d, down).wait_recv()
                when(d < r, lambda: chunk(above, d, down).start())
                when(d == r, lambda: relay(above).start())

            when((above < readers) & (d <= r), take)

        def row_below():
            row(below, 0, up).wait_recv()
            when(r < readers - 1, lambda: row(below, 0, up).start())

        def row_above():
            row(above, 1, down).wait_recv()
            when(r > 0, lambda: row(above, 1, down).start())

        def both(j):
            from_below(j)
            from_above(j)

        each(readers, both)
        when(below >= 0, row_below)
        when(above < readers, row_above)

    each(readers - 1, arrive)
    known_copy = pltpu.make_async_copy(counts, known, known_sem)
    known_copy.start()
    each(readers, lambda s: relay(s).wait_recv())
    known_copy.wait()

    number = [known[q, 0, r] for q in range(readers)]
    base = [jnp.int32(0)]
    for q in range(readers):
        base.append(base[-1] + number[q])
    live = jnp.minimum(base[readers], frames)

    x0[:HALO] = jnp.zeros((HALO, 32, 128), jnp.float32)
    for j in range(frames):
        of, at = jnp.int32(0), jnp.int32(j)
        for q in range(1, readers):
            past = j >= base[q]
            of = jnp.where(past, q, of)
            at = jnp.where(past, j - base[q], at)
        at = jnp.minimum(at, cap - 1)
        mine = box[of, r, at].astype(jnp.float32)
        theirs = other[of, at].astype(jnp.float32)
        a = jnp.where(c == 0, mine, theirs)
        b = jnp.where(c == 0, theirs, mine)
        whole = jnp.concatenate(
            [
                jnp.concatenate([a[:, :64], b[:, :64]], axis=1),
                jnp.concatenate([a[:, 64:], b[:, 64:]], axis=1),
            ],
            axis=0,
        )
        x0[HALO + j] = jnp.where(j < live, whole, 0.0)

    carry = remote(tail_out, tail_in, tail_send, tail_recv, later)

    def take_tail():
        carry.wait_recv()
        x0[:HALO] = tail_in[...].astype(jnp.float32)

    def give_tail():
        when(p > 0, take_tail)
        for i in range(HALO):
            tail_out[i] = x0[live + i].astype(jnp.bfloat16)
        carry.start()

    when(p < periods - 1, give_tail)

    def conv(taps, weights, at, n):
        acc = None
        for t in range(3):
            rows = pl.ds((at + 2 - t) * 32, n * 32)
            part = jnp.dot(taps[rows, :], weights[t], preferred_element_type=jnp.float32)
            acc = part if acc is None else acc + part
        return acc

    def enter(at, n):
        spread(normalize(x0[at : at + n].reshape(n * 32, 128)), taps_a, at, n)

    def middle(at, n):
        hidden = conv(taps_a, first, at, n).astype(jnp.bfloat16).astype(jnp.float32)
        spread(normalize(hidden), taps_b, at, n)

    for at in range(HALO, HALO + frames, 8):
        enter(at, 8)
    weight_loads[0].wait()
    at = 4
    while at < frames + 2:
        n = min(frames + 2 - at, 6 if at == 4 else 8)
        middle(at, n)
        at += n
    when(p == periods - 1, take_tail)
    enter(0, HALO)
    middle(0, 4)

    weight_loads[1].wait()
    for at in range(0, frames, 8):
        update = conv(taps_b, second, at, 8)
        y = x0[HALO + at : HALO + at + 8].reshape(256, 128) + update
        y = jnp.where(c == 0, y[:, :64], y[:, 64:])
        total[at : at + 8] = y.reshape(8, 32, 64)

    for q in range(readers):
        for k in range(cap):
            y = total[jnp.minimum(base[q] + k, frames - 1)]
            y = jnp.where(k < number[q], y, 0.0)
            out[0, q * cap + k] = y.reshape(4, 8, 64).astype(jnp.bfloat16)

    def sent(s):
        def one(d):
            when((s <= r) & (d > r), lambda: chunk(s, d, up).wait_send())
            when((s >= r) & (d < r), lambda: chunk(s, d, down).wait_send())

        each(readers, one)
        when((s <= r) & (r < readers - 1), lambda: row(s, 0, up).wait_send())
        when((s >= r) & (r > 0), lambda: row(s, 1, down).wait_send())
        relay(s).wait_send()

    each(readers, sent)
    when(p < periods - 1, carry.wait_send)


def normalize(values):
    meansq = jnp.mean(values * values, axis=-1, keepdims=True)
    v = values * lax.rsqrt(meansq + EPSILON)
    return v / (1.0 + jnp.exp(-v))


def spread(values, target, first, frames):
    x = values.reshape(frames * 4, 8, 128)
    column = lax.broadcasted_iota(jnp.int32, (1, 8, 128), 1)
    shifted = [
        jnp.where(column == 0, 0.0, pltpu.roll(x, 1, 1)),
        x,
        jnp.where(column == 7, 0.0, pltpu.roll(x, 7, 1)),
    ]
    blank = jnp.zeros((frames, 1, 8, 128), jnp.float32)
    rows = pl.ds(first * 32, frames * 32)
    for v in range(3):
        y = shifted[v].reshape(frames, 4, 8, 128)
        lines = [
            jnp.concatenate([blank, y[:, :3]], axis=1),
            y,
            jnp.concatenate([y[:, 1:], blank], axis=1),
        ]
        for u in range(3):
            tap = u * 3 + v
            target[rows, tap * 128 : (tap + 1) * 128] = (
                lines[u].reshape(frames * 32, 128).astype(jnp.bfloat16)
            )


def body(video, frame_owner, conv_first, conv_second):
    readers = lax.axis_size("clips")
    periods = lax.axis_size("tm")
    slots = video.shape[1]
    cap = max(2, 2 * slots // readers)
    frames = readers * cap
    sizes = (readers, periods, slots, cap)
    vmem = pl.BlockSpec(memory_space=pltpu.VMEM)
    hbm = pl.BlockSpec(memory_space=pltpu.HBM)
    dma = pltpu.SemaphoreType.DMA
    return pl.pallas_call(
        functools.partial(block_kernel, sizes),
        out_shape=jax.ShapeDtypeStruct((1, frames, 4, 8, 64), jnp.bfloat16),
        in_specs=[hbm] * 4,
        out_specs=vmem,
        scratch_shapes=[
            pltpu.VMEM((readers, readers, cap, 16, 128), jnp.bfloat16),
            pltpu.VMEM((readers, cap, 16, 128), jnp.bfloat16),
            pltpu.VMEM((HALO, 32, 128), jnp.bfloat16),
            pltpu.VMEM((HALO, 32, 128), jnp.bfloat16),
            pltpu.VMEM((readers, 1, 128), jnp.int32),
            pltpu.SMEM((readers, 1, 128), jnp.int32),
            pltpu.VMEM((3, 1152, 128), jnp.bfloat16),
            pltpu.VMEM((3, 1152, 128), jnp.bfloat16),
            pltpu.VMEM((frames + HALO, 32, 128), jnp.float32),
            pltpu.VMEM(((frames + HALO) * 32, 1152), jnp.bfloat16),
            pltpu.VMEM(((frames + 2) * 32, 1152), jnp.bfloat16),
            pltpu.VMEM((frames, 32, 64), jnp.float32),
            pltpu.SMEM((1, slots), jnp.int32),
            pltpu.VMEM((slots, 4, 8, 64), jnp.bfloat16),
            pltpu.VMEM((slots, 16, 128), jnp.bfloat16),
            pltpu.SMEM((readers * 32,), jnp.int32),
            dma,
            dma,
            dma,
            dma((2,)),
            dma((readers * readers,)),
            dma((readers * readers,)),
            dma((2 * readers,)),
            dma((readers,)),
            dma((readers,)),
            dma((readers,)),
            dma,
            dma,
        ],
        compiler_params=pltpu.CompilerParams(
            collective_id=0, has_side_effects=True, vmem_limit_bytes=60 * 2**20
        ),
    )(
        video,
        frame_owner.reshape(1, slots),
        conv_first.reshape(3, 1152, 128),
        conv_second.reshape(3, 1152, 128),
    )


def solution(mesh):
    placed = (
        P(("groups", "tm"), "clips", None, None, "chan"),
        P(("groups", "tm"), "clips", None),
        P(),
        P(),
    )
    return jax.shard_map(
        body,
        mesh=mesh,
        in_specs=placed,
        out_specs=P(("groups", "tm"), "clips", None, None, "chan"),
        check_vma=False,
    )
```

```python
import functools

import jax
import jax.numpy as jnp
from jax import lax
from jax.experimental import pallas as pl
from jax.experimental.pallas import tpu as pltpu
from jax.sharding import PartitionSpec as P

EPSILON = 1e-06
MESH = pl.DeviceIdType.MESH
HALO = 4


def each(count, step):
    if count <= 8:
        for i in range(count):
            step(i)
    else:
        lax.fori_loop(0, count, lambda i, c: (step(i), c)[1], 0)


def block_kernel(
    sizes, video, owner_rows, first_in, second_in, out,
    box, other, tail_in, tail_out, counts, known, first, second, x0, taps_a, taps_b, total,
    owners, raw, packed, after,
    known_sem, load_sem, owner_sem, weight_sem, send_sem, recv_sem, count_send, count_recv,
    pass_send, pass_recv, tail_send, tail_recv,
):
    readers, periods, slots, cap = sizes
    frames = readers * cap
    g = lax.axis_index("groups")
    r = lax.axis_index("clips")
    p = lax.axis_index("tm")
    c = lax.axis_index("chan")
    load = pltpu.make_async_copy(video.at[0], raw, load_sem)
    name_load = pltpu.make_async_copy(owner_rows, owners, owner_sem)
    name_load.start()
    load.start()
    weight_loads = [
        pltpu.make_async_copy(first_in, first, weight_sem.at[0]),
        pltpu.make_async_copy(second_in, second, weight_sem.at[1]),
    ]
    later = (g, r, p + 1, c)
    earlier = (g, r, p - 1, c)
    sibling = (g, r, p, 1 - c)

    barrier = pltpu.get_barrier_semaphore()

    def greet(there, who):
        @pl.when(there)
        def _():
            pl.semaphore_signal(barrier, inc=1, device_id=who, device_id_type=MESH)

    def greet_clip(i):
        to = (g, lax.rem(r + i + 1, readers), p, c)
        pl.semaphore_signal(barrier, inc=1, device_id=to, device_id_type=MESH)

    each(readers - 1, greet_clip)
    greet(p < periods - 1, later)
    greet(p > 0, earlier)
    pl.semaphore_signal(barrier, inc=1, device_id=sibling, device_id_type=MESH)
    for d in weight_loads:
        d.start()

    name_load.wait()
    lane = lax.broadcasted_iota(jnp.int32, (1, 128), 1)
    tally = jnp.zeros((1, 128), jnp.int32)
    names = [owners[0, s] for s in range(slots)]
    for s in range(slots):
        tally = tally + jnp.where(lane == names[s], 1, 0)
    counts[r] = tally

    def tables(o):
        base = o * 32
        n = jnp.int32(slots)
        after[base + slots] = n
        after[base + slots + 1] = n
        for s in reversed(range(slots)):
            n = jnp.where(names[s] == o, s, n)
            after[base + s] = n

    each(readers, tables)

    load.wait()
    for s in range(slots):
        v = raw[s].astype(jnp.float32).reshape(32, 64)
        packed[s] = jnp.concatenate([v[:16], v[16:]], axis=1).astype(jnp.bfloat16)

    def pack(o):
        s = after[o * 32]
        for k in range(cap):
            box[r, o, k] = packed[jnp.minimum(s, slots - 1)]
            s = after[o * 32 + s + 1]

    each(readers, pack)
    neighbours = (
        readers
        + jnp.where(p < periods - 1, 1, 0)
        + jnp.where(p > 0, 1, 0)
    )
    pl.semaphore_wait(barrier, neighbours)

    def remote(source, target, sent, got, who):
        return pltpu.make_async_remote_copy(
            source, target, sent, got, device_id=who, device_id_type=MESH)

    def chunk(s, d, who):
        to = (g, who, p, c)
        return (
            remote(box.at[s, d], box.at[s, d], send_sem.at[d], recv_sem.at[s], to),
            remote(counts.at[s], counts.at[s], count_send.at[d], count_recv.at[s], to),
        )

    def relay(s):
        return remote(box.at[s, r], other.at[s], pass_send.at[s], pass_recv.at[s], sibling)

    def when(there, act):
        @pl.when(there)
        def _():
            act()

    def partner(i):
        return lax.rem(r + 1 + lax.rem(readers // 2 - 1 + i, readers - 1), readers)

    def start_chunks(i):
        for d in chunk(r, partner(i), partner(i)):
            d.start()

    each(readers - 1, start_chunks)
    relay(r).start()

    def arrive(i):
        def take(s):
            for d in chunk(s, r, s):
                d.wait_recv()
            relay(s).start()

        when(r >= 1 + i, lambda: take(r - 1 - i))
        when(r + 1 + i < readers, lambda: take(r + 1 + i))

    each(readers - 1, arrive)
    known_copy = pltpu.make_async_copy(counts, known, known_sem)
    known_copy.start()
    each(readers, lambda s: relay(s).wait_recv())
    known_copy.wait()

    number = [known[q, 0, r] for q in range(readers)]
    base = [jnp.int32(0)]
    for q in range(readers):
        base.append(base[-1] + number[q])
    live = jnp.minimum(base[readers], frames)

    x0[:HALO] = jnp.zeros((HALO, 32, 128), jnp.float32)
    for j in range(frames):
        of, at = jnp.int32(0), jnp.int32(j)
        for q in range(1, readers):
            past = j >= base[q]
            of = jnp.where(past, q, of)
            at = jnp.where(past, j - base[q], at)
        at = jnp.minimum(at, cap - 1)
        mine = box[of, r, at].astype(jnp.float32)
        theirs = other[of, at].astype(jnp.float32)
        a = jnp.where(c == 0, mine, theirs)
        b = jnp.where(c == 0, theirs, mine)
        whole = jnp.concatenate(
            [
                jnp.concatenate([a[:, :64], b[:, :64]], axis=1),
                jnp.concatenate([a[:, 64:], b[:, 64:]], axis=1),
            ],
            axis=0,
        )
        x0[HALO + j] = jnp.where(j < live, whole, 0.0)

    carry = remote(tail_out, tail_in, tail_send, tail_recv, later)

    def take_tail():
        carry.wait_recv()
        x0[:HALO] = tail_in[...].astype(jnp.float32)

    def give_tail():
        when(p > 0, take_tail)
        for i in range(HALO):
            tail_out[i] = x0[live + i].astype(jnp.bfloat16)
        carry.start()

    when(p < periods - 1, give_tail)

    def conv(taps, weights, at, n):
        acc = None
        for t in range(3):
            rows = pl.ds((at + 2 - t) * 32, n * 32)
            part = jnp.dot(taps[rows, :], weights[t], preferred_element_type=jnp.float32)
            acc = part if acc is None else acc + part
        return acc

    def enter(at, n):
        spread(normalize(x0[at : at + n].reshape(n * 32, 128)), taps_a, at, n)

    def middle(at, n):
        hidden = conv(taps_a, first, at, n).astype(jnp.bfloat16).astype(jnp.float32)
        spread(normalize(hidden), taps_b, at, n)

    for at in range(HALO, HALO + frames, 8):
        enter(at, 8)
    weight_loads[0].wait()
    at = 4
    while at < frames + 2:
        n = min(frames + 2 - at, 6 if at == 4 else 8)
        middle(at, n)
        at += n
    when(p == periods - 1, take_tail)
    enter(0, HALO)
    middle(0, 4)

    weight_loads[1].wait()
    for at in range(0, frames, 8):
        update = conv(taps_b, second, at, 8)
        y = x0[HALO + at : HALO + at + 8].reshape(256, 128) + update
        y = jnp.where(c == 0, y[:, :64], y[:, 64:])
        total[at : at + 8] = y.reshape(8, 32, 64)

    for q in range(readers):
        for k in range(cap):
            y = total[jnp.minimum(base[q] + k, frames - 1)]
            y = jnp.where(k < number[q], y, 0.0)
            out[0, q * cap + k] = y.reshape(4, 8, 64).astype(jnp.bfloat16)

    def sent(i):
        for d in chunk(r, partner(i), partner(i)):
            d.wait_send()

    each(readers - 1, sent)
    each(readers, lambda s: relay(s).wait_send())
    when(p < periods - 1, carry.wait_send)


def normalize(values):
    meansq = jnp.mean(values * values, axis=-1, keepdims=True)
    v = values * lax.rsqrt(meansq + EPSILON)
    return v / (1.0 + jnp.exp(-v))


def spread(values, target, first, frames):
    x = values.reshape(frames * 4, 8, 128)
    column = lax.broadcasted_iota(jnp.int32, (1, 8, 128), 1)
    shifted = [
        jnp.where(column == 0, 0.0, pltpu.roll(x, 1, 1)),
        x,
        jnp.where(column == 7, 0.0, pltpu.roll(x, 7, 1)),
    ]
    blank = jnp.zeros((frames, 1, 8, 128), jnp.float32)
    rows = pl.ds(first * 32, frames * 32)
    for v in range(3):
        y = shifted[v].reshape(frames, 4, 8, 128)
        lines = [
            jnp.concatenate([blank, y[:, :3]], axis=1),
            y,
            jnp.concatenate([y[:, 1:], blank], axis=1),
        ]
        for u in range(3):
            tap = u * 3 + v
            target[rows, tap * 128 : (tap + 1) * 128] = (
                lines[u].reshape(frames * 32, 128).astype(jnp.bfloat16)
            )


def body(video, frame_owner, conv_first, conv_second):
    readers = lax.axis_size("clips")
    periods = lax.axis_size("tm")
    slots = video.shape[1]
    cap = max(2, 2 * slots // readers)
    frames = readers * cap
    sizes = (readers, periods, slots, cap)
    vmem = pl.BlockSpec(memory_space=pltpu.VMEM)
    hbm = pl.BlockSpec(memory_space=pltpu.HBM)
    dma = pltpu.SemaphoreType.DMA
    return pl.pallas_call(
        functools.partial(block_kernel, sizes),
        out_shape=jax.ShapeDtypeStruct((1, frames, 4, 8, 64), jnp.bfloat16),
        in_specs=[hbm] * 4,
        out_specs=vmem,
        scratch_shapes=[
            pltpu.VMEM((readers, readers, cap, 16, 128), jnp.bfloat16),
            pltpu.VMEM((readers, cap, 16, 128), jnp.bfloat16),
            pltpu.VMEM((HALO, 32, 128), jnp.bfloat16),
            pltpu.VMEM((HALO, 32, 128), jnp.bfloat16),
            pltpu.VMEM((readers, 1, 128), jnp.int32),
            pltpu.SMEM((readers, 1, 128), jnp.int32),
            pltpu.VMEM((3, 1152, 128), jnp.bfloat16),
            pltpu.VMEM((3, 1152, 128), jnp.bfloat16),
            pltpu.VMEM((frames + HALO, 32, 128), jnp.float32),
            pltpu.VMEM(((frames + HALO) * 32, 1152), jnp.bfloat16),
            pltpu.VMEM(((frames + 2) * 32, 1152), jnp.bfloat16),
            pltpu.VMEM((frames, 32, 64), jnp.float32),
            pltpu.SMEM((1, slots), jnp.int32),
            pltpu.VMEM((slots, 4, 8, 64), jnp.bfloat16),
            pltpu.VMEM((slots, 16, 128), jnp.bfloat16),
            pltpu.SMEM((readers * 32,), jnp.int32),
            dma,
            dma,
            dma,
            dma((2,)),
            dma((readers,)),
            dma((readers,)),
            dma((readers,)),
            dma((readers,)),
            dma((readers,)),
            dma((readers,)),
            dma,
            dma,
        ],
        compiler_params=pltpu.CompilerParams(
            collective_id=0, has_side_effects=True, vmem_limit_bytes=60 * 2**20
        ),
    )(
        video,
        frame_owner.reshape(1, slots),
        conv_first.reshape(3, 1152, 128),
        conv_second.reshape(3, 1152, 128),
    )


def solution(mesh):
    placed = (
        P(("groups", "tm"), "clips", None, None, "chan"),
        P(("groups", "tm"), "clips", None),
        P(),
        P(),
    )
    return jax.shard_map(
        body,
        mesh=mesh,
        in_specs=placed,
        out_specs=P(("groups", "tm"), "clips", None, None, "chan"),
        check_vma=False,
    )
```
